512 devices in a mesh: seq: 64 (over y, z), cand: 8 (over x, core).
Axes of the slice: x: 4, y: 4, z: 16, core: 2. Of those that a mesh axis runs over, the one named last changes fastest.
Arguments:
- candidates: bfloat16 [2, 1024, 256], P(None, ('seq', 'cand')), may hold values from -30 to 30
- history: bfloat16 [2, 65536, 256], P(None, ('seq', 'cand')), may hold values from -30 to 30
- lengths: int32 [2], replicated, may hold values from 6553 to 65536, as said below
- w_query: bfloat16 [256, 256], replicated, may hold values from -0.525 to 0.525
- w_key: bfloat16 [256, 256], replicated, may hold values from -0.525 to 0.525
- w_value: bfloat16 [256, 256], replicated, may hold values from -0.375 to 0.375
- norm_gain: float32 [256], replicated, may hold values from 0.3 to 3
- w_out: bfloat16 [256, 256], replicated, may hold values from -0.375 to 0.375
Outputs:
- interest: bfloat16 [2, 1024, 256], P(None, ('seq', 'cand'))
The draws below stay inside these ranges and needn't reach their ends.
Inputs may be any that keep to these rules, and one draw needn't show every extreme that they name: User u's valid history is its first lengths[u] slots; some user fills all 65536.
All inputs are finite; a program needn't handle non-finite values.
Results may differ from the reference program's by a relative error of at most 0.019.
Values may be sent and summed in bfloat16 or wider, within the bound.
No kernel may reach another device: no remote copies, remote signals or barrier semaphores. Data moves between devices by JAX's collectives and lax.ppermute only.
A program may use at most 64 MiB of HBM per device.

```python
import math
import jax
import jax.numpy as jnp
from jax import lax

D = 256
HEADS = 8
HEAD_DIM = 32
USERS = 2
CANDS = 1024
MAXLEN = 65536


def shared_matrix(key):
    return jnp.clip(jax.random.normal(jax.random.fold_in(key, 11), (D, HEADS * HEAD_DIM), jnp.float32), -6.0, 6.0)


def drawn_rows(key, shape):
    first_key = jax.random.fold_in(key, 0)
    return jnp.clip(jax.random.normal(first_key, shape, jnp.float32), -6.0, 6.0)


def draw_candidates(key, part):
    key = jax.random.fold_in(key, 1)
    return drawn_rows(key, (USERS, CANDS, D)).astype(jnp.bfloat16)


def draw_history(key, part):
    key = jax.random.fold_in(key, 2)
    return drawn_rows(key, (USERS, MAXLEN, D)).astype(jnp.bfloat16)


def draw_lengths(key, part):
    key = jax.random.fold_in(key, 3)
    first_key, second_key = jax.random.split(key)
    sampled = jax.random.randint(first_key, (USERS,), MAXLEN // 10, MAXLEN + 1, dtype=jnp.int32)
    longest = jax.random.randint(second_key, (), 0, USERS, dtype=jnp.int32)
    return jnp.where(jnp.arange(USERS, dtype=jnp.int32) == longest, MAXLEN, sampled).astype(jnp.int32)


def draw_w_query(key, part):
    common = shared_matrix(key)
    key = jax.random.fold_in(key, 4)
    private = jnp.clip(jax.random.normal(key, (D, HEADS * HEAD_DIM), jnp.float32), -6.0, 6.0)
    return ((0.8 * common + 0.6 * private) * D ** (-0.5)).astype(jnp.bfloat16)


def draw_w_key(key, part):
    common = shared_matrix(key)
    key = jax.random.fold_in(key, 5)
    private = jnp.clip(jax.random.normal(key, (D, HEADS * HEAD_DIM), jnp.float32), -6.0, 6.0)
    return ((0.8 * common + 0.6 * private) * D ** (-0.5)).astype(jnp.bfloat16)


def centred(own_key, extent, deviation, bound, held_as=jnp.bfloat16):
    array = jax.random.normal(own_key, extent, jnp.float32) * deviation
    return jnp.minimum(jnp.maximum(array, -bound), bound).astype(held_as)


def setup_inputs(seed: int = 0) -> dict:
    splits = jax.random.split(jax.random.key(seed), 9)
    return {
        "candidates": draw_candidates(jax.random.fold_in(splits[8], 71), 0),
        "history": draw_history(jax.random.fold_in(splits[8], 71), 0),
        "lengths": draw_lengths(jax.random.fold_in(splits[8], 71), 0),
        "w_query": draw_w_query(jax.random.fold_in(splits[8], 71), 0),
        "w_key": draw_w_key(jax.random.fold_in(splits[8], 71), 0),
        "w_value": centred(splits[5], (D, HEADS * HEAD_DIM), D ** -0.5, 0.375),
        "norm_gain": jnp.clip(jnp.exp(jax.random.uniform(splits[6], (HEADS * HEAD_DIM,), jnp.float32, math.log(0.3), math.log(3.0))), 0.3, 3.0),
        "w_out": centred(splits[7], (HEADS * HEAD_DIM, D), (HEADS * HEAD_DIM) ** -0.5, 0.375),
    }


def reference(candidates, history, lengths, w_query, w_key, w_value, norm_gain, w_out):
    inner_width = HEADS * HEAD_DIM
    queries = jnp.dot(candidates.reshape(USERS * CANDS, D), w_query, preferred_element_type=jnp.float32)
    queries = queries.astype(jnp.bfloat16).reshape(USERS, CANDS, HEADS, HEAD_DIM)
    flat_history = history.reshape(USERS * MAXLEN, D)
    keys = jnp.dot(flat_history, w_key, preferred_element_type=jnp.float32)
    keys = keys.astype(jnp.bfloat16).reshape(USERS, MAXLEN, HEADS, HEAD_DIM)
    values = jnp.dot(flat_history, w_value, preferred_element_type=jnp.float32)
    values = values.astype(jnp.bfloat16).reshape(USERS, MAXLEN, HEADS, HEAD_DIM)
    block_size = math.gcd(CANDS, 64)
    positions = jnp.arange(MAXLEN, dtype=jnp.int32)
    score_scale = 1.0 / math.sqrt(HEAD_DIM)

    def per_user(user_items):
        query_user, key_user, value_user, length_user = user_items
        row_valid = (positions < length_user)[None, None, :]
        key_wide = key_user.astype(jnp.float32)
        value_wide = value_user.astype(jnp.float32)

        def per_block(query_block):
            scores = jnp.einsum('chd,rhd->chr', query_block.astype(jnp.float32), key_wide) * score_scale
            scores = jnp.where(row_valid, scores, jnp.float32(-1e+30))
            peaks = lax.optimization_barrier(jnp.max(scores, axis=2))
            exponent = jnp.where(row_valid, jnp.exp(scores - peaks[:, :, None]), jnp.float32(0.0))
            row_total = lax.optimization_barrier(jnp.sum(exponent, axis=2))
            rounded = lax.optimization_barrier(exponent.astype(jnp.bfloat16)).astype(jnp.float32)
            numerator = jnp.einsum('chr,rhd->chd', rounded, value_wide)
            return numerator / row_total[:, :, None]
        blocks = query_user.reshape(CANDS // block_size, block_size, HEADS, HEAD_DIM)
        return lax.map(per_block, blocks).reshape(CANDS, inner_width)
    attended = lax.map(per_user, (queries, keys, values, lengths))
    normed = attended * lax.rsqrt(lax.optimization_barrier(jnp.mean(attended * attended, axis=-1, keepdims=True)) + 1e-06) * norm_gain
    normed = normed.astype(jnp.bfloat16)
    result = jnp.dot(normed.reshape(USERS * CANDS, inner_width), w_out, preferred_element_type=jnp.float32)
    return result.astype(jnp.bfloat16).reshape(USERS, CANDS, D)
```

```python
import functools
import math

import jax
import jax.numpy as jnp
from jax import lax
from jax.experimental import pallas as pl
from jax.experimental.pallas import tpu as pltpu
from jax.sharding import PartitionSpec as P

HEAD_DIM = 32
LANES = 128
SLOT = 16
EXPONENT = math.log2(math.e) / math.sqrt(HEAD_DIM)
NT = (((1,), (1,)), ((), ()))


def parts_of(array, count):
    pieces = []
    for _ in range(count):
        piece = array.astype(jnp.bfloat16).astype(jnp.float32)
        pieces.append(piece)
        array = array - piece
    return pieces


def attend_kernel(
    length_ref, cand_ref, history_ref, wq_ref, wk_ref, wv_ref, out_ref, cand_wide, out_wide
):
    users, rows, width = history_ref.shape
    devices = cand_ref.shape[0] // 8
    own = 2
    heads = width // HEAD_DIM
    cands = devices * own
    first_row = lax.axis_index("seq") * rows
    cand_wide[...] = cand_ref[...].astype(jnp.float32)
    out_wide[...] = jnp.zeros_like(out_wide)
    head_of_lane = lax.broadcasted_iota(jnp.int32, (cands, width), 1) // HEAD_DIM
    row_index = lax.broadcasted_iota(jnp.int32, (rows, width), 0)
    lane_index = lax.broadcasted_iota(jnp.int32, (width, rows), 1)
    for user in range(users):
        valid = length_ref[user] - first_row
        history = history_ref[user]
        keys = jnp.dot(history, wk_ref[...], preferred_element_type=jnp.float32)
        keys = jnp.where(row_index < valid, keys, keys[0:1]).astype(jnp.bfloat16)
        values = lax.dot_general(
            wv_ref[...], history, (((0,), (1,)), ((), ())), preferred_element_type=jnp.float32
        )
        values = jnp.where(lane_index < valid, values, 0.0).astype(jnp.bfloat16)
        ones = jnp.where(lane_index[:16] < valid, 1.0, 0.0).astype(jnp.bfloat16)
        halves = [
            jnp.concatenate(
                [
                    cand_wide[pl.ds((user * own + i) * 2 + half, devices, stride=8), :]
                    for half in range(2)
                ],
                axis=1,
            )
            for i in range(own)
        ]
        candidates = jnp.concatenate(halves, axis=0).astype(jnp.bfloat16)
        queries = jnp.dot(candidates, wq_ref[...], preferred_element_type=jnp.float32)
        queries = queries.astype(jnp.bfloat16).astype(jnp.float32)
        numerators, peaks, totals = [], [], []
        for pair in range(heads // 2):
            both = jnp.concatenate(
                [
                    jnp.where(head_of_lane == 2 * pair + k, queries, 0.0).astype(jnp.bfloat16)
                    for k in range(2)
                ],
                axis=0,
            )
            scores = lax.dot_general(keys, both, NT, preferred_element_type=jnp.float32)
            peak = jnp.max(scores, axis=0, keepdims=True)
            exps = jnp.exp2((scores - peak) * EXPONENT).astype(jnp.bfloat16)
            pair_values = jnp.concatenate(
                [values[2 * pair * HEAD_DIM : 2 * (pair + 1) * HEAD_DIM], ones], axis=0
            )
            sums = jnp.dot(pair_values, exps, preferred_element_type=jnp.float32)
            for k in range(2):
                lanes = slice(k * cands, (k + 1) * cands)
                numerators.append(sums[k * HEAD_DIM : (k + 1) * HEAD_DIM, lanes])
                peaks.append(peak[:, lanes])
                totals.append(sums[2 * HEAD_DIM : 2 * HEAD_DIM + 1, lanes])
        peak = jnp.where(valid > 0, jnp.concatenate(peaks, axis=0), -1e30)
        total = jnp.concatenate(totals, axis=0)
        pieces = parts_of(peak, 3) + parts_of(total, 2)
        filler = jnp.zeros((LANES - len(pieces) * heads, cands), jnp.float32)
        block = jnp.concatenate(numerators + pieces + [filler], axis=0)
        for part in range(3):
            turned = block[part * LANES : (part + 1) * LANES].T
            for i in range(own):
                out_wide[pl.ds((user * own + i) * 3 + part, devices, stride=SLOT), :] = turned[
                    i * devices : (i + 1) * devices
                ]
    out_ref[...] = out_wide[...].astype(jnp.bfloat16)


def join_kernel(part_ref, gain_ref, wout_ref, out_ref, wide):
    width = wout_ref.shape[0]
    heads = width // HEAD_DIM
    devices = part_ref.shape[0] // SLOT
    own_count = out_ref.shape[0]
    wide[...] = part_ref[...].astype(jnp.float32)

    def rows(own, part):
        return wide[pl.ds(own * 3 + part, devices, stride=SLOT), :]

    lane = lax.broadcasted_iota(jnp.int32, (LANES, 2 * width), 0)
    column = lax.broadcasted_iota(jnp.int32, (LANES, 2 * width), 1)
    is_peak = column < width
    head = jnp.where(is_peak, column, column - width) // HEAD_DIM
    same = (lane % heads == head) & (
        (is_peak & (lane < 3 * heads))
        | (~is_peak & (lane >= 3 * heads) & (lane < 5 * heads))
    )
    spread = jnp.where(same, 1.0, 0.0).astype(jnp.bfloat16)
    stats = jnp.concatenate([rows(own, 2) for own in range(own_count)], axis=0)
    stats = jnp.dot(stats.astype(jnp.bfloat16), spread, preferred_element_type=jnp.float32)
    attended = []
    for own in range(own_count):
        peak = stats[own * devices : (own + 1) * devices, :width]
        total = stats[own * devices : (own + 1) * devices, width:]
        joint = jnp.max(peak, axis=0, keepdims=True)
        factor = jnp.exp2((peak - joint) * EXPONENT)
        numerator = jnp.concatenate([rows(own, 0), rows(own, 1)], axis=1)
        numerator = jnp.sum(numerator * factor, axis=0, keepdims=True)
        attended.append(numerator / jnp.sum(total * factor, axis=0, keepdims=True))
    attended = jnp.concatenate(attended, axis=0)
    normed = (
        attended
        * lax.rsqrt(jnp.mean(attended * attended, axis=-1, keepdims=True) + 1e-06)
        * gain_ref[...]
    )
    out_ref[...] = jnp.dot(
        normed.astype(jnp.bfloat16), wout_ref[...], preferred_element_type=jnp.float32
    ).astype(jnp.bfloat16)


def shards(seq_count, candidates, history, lengths, w_query, w_key, w_value, norm_gain, w_out):
    users, own, width = candidates.shape
    vmem = pl.BlockSpec(memory_space=pltpu.VMEM)
    smem = pl.BlockSpec(memory_space=pltpu.SMEM)
    rows = lax.all_gather(history, "cand", axis=1, tiled=True)
    copies = jnp.broadcast_to(candidates.reshape(1, 8, LANES), (seq_count, 8, LANES))
    gathered = lax.all_to_all(copies, "seq", 0, 0, tiled=True).reshape(seq_count * 8, LANES)
    partial = pl.pallas_call(
        attend_kernel,
        out_shape=jax.ShapeDtypeStruct((seq_count * SLOT, LANES), jnp.bfloat16),
        in_specs=[smem] + [vmem] * 5,
        out_specs=vmem,
        scratch_shapes=[
            pltpu.VMEM((seq_count * 8, LANES), jnp.float32),
            pltpu.VMEM((seq_count * SLOT, LANES), jnp.float32),
        ],
        compiler_params=pltpu.CompilerParams(vmem_limit_bytes=48 * 1024 * 1024),
        name="attend",
    )(lengths, gathered, rows, w_query, w_key, w_value)
    partial = lax.all_to_all(partial.reshape(seq_count, SLOT, LANES), "seq", 0, 0, tiled=True)
    result = pl.pallas_call(
        join_kernel,
        out_shape=jax.ShapeDtypeStruct((users * own, width), jnp.bfloat16),
        in_specs=[vmem] * 3,
        out_specs=vmem,
        scratch_shapes=[pltpu.VMEM((seq_count * SLOT, LANES), jnp.float32)],
        compiler_params=pltpu.CompilerParams(vmem_limit_bytes=16 * 1024 * 1024),
        name="join",
    )(partial.reshape(seq_count * SLOT, LANES), norm_gain.reshape(1, width), w_out)
    return result.reshape(users, own, width)


def solution(mesh):
    split = P(None, ("seq", "cand"), None)
    return jax.shard_map(
        functools.partial(shards, mesh.shape["seq"]),
        mesh=mesh,
        in_specs=(split, split) + (P(),) * 6,
        out_specs=split,
        check_vma=False,
    )
```

```python
import functools
import math

import jax
import jax.numpy as jnp
from jax import lax
from jax.experimental import pallas as pl
from jax.experimental.pallas import tpu as pltpu
from jax.sharding import Mesh, PartitionSpec as P

HEAD_DIM = 32
LANES = 128
SLOT = 10
STATS = 64
EXPONENT = math.log2(math.e) / math.sqrt(HEAD_DIM)
NT = (((1,), (1,)), ((), ()))
ONES = 16


def parts_of(array, count):
    pieces = []
    for _ in range(count):
        piece = array.astype(jnp.bfloat16).astype(jnp.float32)
        pieces.append(piece)
        array = array - piece
    return pieces


def project_kernel(side, length_ref, *refs):
    history_refs, (wk_ref, wv_ref, keys_ref, values_ref) = refs[:-4], refs[-4:]
    chips, users, block, width = history_refs[0].shape
    rows = len(history_refs) * chips * block
    first_row = lax.axis_index("seq") * 2 * rows
    core = (lax.axis_index("core") + side) % 2

    def position(shape, dimension):
        index = lax.broadcasted_iota(jnp.int32, shape, dimension)
        return (index // block) * (2 * block) + core * block + index % block

    row_index = position((rows, width), 0)
    lane_index = position((width + ONES, rows), 1)
    for user in range(users):
        valid = length_ref[user] - first_row
        history = jnp.concatenate(
            [ref[:, user].reshape(chips * block, width) for ref in history_refs], axis=0
        )
        keys = jnp.dot(history, wk_ref[...], preferred_element_type=jnp.float32)
        keys_ref[user] = jnp.where(row_index < valid, keys, keys[0:1]).astype(jnp.bfloat16)
        values = lax.dot_general(
            wv_ref[...], history, (((0,), (1,)), ((), ())), preferred_element_type=jnp.float32
        )
        values = jnp.concatenate([values, jnp.ones((ONES, rows), jnp.float32)], axis=0)
        values_ref[user] = jnp.where(lane_index < valid, values, 0.0).astype(jnp.bfloat16)


def attend_kernel(cand_ref, keys0, values0, keys1, values1, wq_ref, out_ref, cand_wide, out_wide):
    users, _, width = keys0.shape
    devices = cand_ref.shape[0] // 8
    own = 2
    heads = width // HEAD_DIM
    cands = devices * own
    cand_wide[...] = cand_ref[...].astype(jnp.float32)
    head_of_lane = lax.broadcasted_iota(jnp.int32, (cands, width), 1) // HEAD_DIM
    for user in range(users):
        halves = [(keys0, values0), (keys1, values1)]
        any_valid = [values[user, width : width + 1, 0:1] > 0.0 for _, values in halves]
        keys = [
            jnp.where(any_valid[k], halves[k][0][user], halves[1 - k][0][user, 0:1])
            for k in range(2)
        ]
        candidates = [
            jnp.concatenate(
                [
                    cand_wide[pl.ds((user * own + i) * 2 + half, devices, stride=8), :]
                    for half in range(2)
                ],
                axis=1,
            )
            for i in range(own)
        ]
        candidates = jnp.concatenate(candidates, axis=0).astype(jnp.bfloat16)
        queries = jnp.dot(candidates, wq_ref[...], preferred_element_type=jnp.float32)
        queries = queries.astype(jnp.bfloat16).astype(jnp.float32)
        numerators, peaks, totals = [], [], []
        for pair in range(heads // 2):
            both = jnp.concatenate(
                [
                    jnp.where(head_of_lane == 2 * pair + k, queries, 0.0).astype(jnp.bfloat16)
                    for k in range(2)
                ],
                axis=0,
            )
            scores = [
                lax.dot_general(part, both, NT, preferred_element_type=jnp.float32)
                for part in keys
            ]
            peak = jnp.max(jnp.maximum(scores[0], scores[1]), axis=0, keepdims=True)
            sums = 0.0
            for part, (_, values) in zip(scores, halves):
                exps = jnp.exp2((part - peak) * EXPONENT).astype(jnp.bfloat16)
                pair_values = jnp.concatenate(
                    [
                        values[user, 2 * pair * HEAD_DIM : 2 * (pair + 1) * HEAD_DIM],
                        values[user, width:],
                    ],
                    axis=0,
                )
                sums += jnp.dot(pair_values, exps, preferred_element_type=jnp.float32)
            for k in range(2):
                lanes = slice(k * cands, (k + 1) * cands)
                numerators.append(sums[k * HEAD_DIM : (k + 1) * HEAD_DIM, lanes])
                peaks.append(peak[:, lanes])
                totals.append(sums[2 * HEAD_DIM : 2 * HEAD_DIM + 1, lanes])
        total = jnp.concatenate(totals, axis=0)
        peak = jnp.where(total > 0.0, jnp.concatenate(peaks, axis=0), -1e30)
        pieces = parts_of(peak, 3) + parts_of(total, 2)
        filler = jnp.zeros((STATS - len(pieces) * heads, cands), jnp.float32)
        block = jnp.concatenate(numerators, axis=0)
        for half in range(2):
            turned = block[half * LANES : (half + 1) * LANES].T
            for i in range(own):
                row = (user * own + i) * 2 + half
                out_wide[pl.ds(row, devices, stride=SLOT), :] = turned[
                    i * devices : (i + 1) * devices
                ]
        stats = jnp.concatenate(pieces + [filler], axis=0)
        stats = jnp.concatenate(
            [stats[:, i * devices : (i + 1) * devices] for i in range(own)], axis=0
        )
        out_wide[pl.ds(2 * users * own + user, devices, stride=SLOT), :] = stats.T
    out_ref[...] = out_wide[...].astype(jnp.bfloat16)


def join_kernel(part_ref, gain_ref, wout_ref, out_ref, wide):
    width = wout_ref.shape[0]
    heads = width // HEAD_DIM
    devices = part_ref.shape[0] // SLOT
    users, own = out_ref.shape[:2]
    own_count = users * own
    wide[...] = part_ref[...].astype(jnp.float32)

    def rows(index):
        return wide[pl.ds(index, devices, stride=SLOT), :]

    lane = lax.broadcasted_iota(jnp.int32, (LANES, 2 * own * width), 0)
    column = lax.broadcasted_iota(jnp.int32, (LANES, 2 * own * width), 1)
    piece = lane % STATS // heads
    is_total = column // width % 2
    same = (
        (lane // STATS == column // (2 * width))
        & (lane % heads == column % width // HEAD_DIM)
        & (piece >= 3 * is_total)
        & (piece < 3 + 2 * is_total)
    )
    spread = jnp.where(same, 1.0, 0.0).astype(jnp.bfloat16)
    stats = jnp.concatenate([rows(2 * own_count + user) for user in range(users)], axis=0)
    stats = jnp.dot(stats.astype(jnp.bfloat16), spread, preferred_element_type=jnp.float32)
    attended = []
    for user in range(users):
        for i in range(own):
            both = stats[user * devices : (user + 1) * devices]
            peak = both[:, 2 * i * width : (2 * i + 1) * width]
            total = both[:, (2 * i + 1) * width : (2 * i + 2) * width]
            joint = jnp.max(peak, axis=0, keepdims=True)
            factor = jnp.exp2((peak - joint) * EXPONENT)
            index = 2 * (user * own + i)
            numerator = jnp.concatenate([rows(index), rows(index + 1)], axis=1)
            numerator = jnp.sum(numerator * factor, axis=0, keepdims=True)
            attended.append(numerator / jnp.sum(total * factor, axis=0, keepdims=True))
    attended = jnp.concatenate(attended, axis=0)
    normed = (
        attended
        * lax.rsqrt(jnp.mean(attended * attended, axis=-1, keepdims=True) + 1e-06)
        * gain_ref[...]
    )
    result = jnp.dot(
        normed.astype(jnp.bfloat16), wout_ref[...], preferred_element_type=jnp.float32
    )
    for user in range(users):
        out_ref[user] = result[user * own : (user + 1) * own].astype(jnp.bfloat16)


def shards(seq_count, candidates, history, lengths, w_query, w_key, w_value, norm_gain, w_out):
    users, own, width = candidates.shape
    vmem = pl.BlockSpec(memory_space=pltpu.VMEM)
    smem = pl.BlockSpec(memory_space=pltpu.SMEM)
    copies = jnp.broadcast_to(candidates.reshape(1, 8, LANES), (seq_count, 8, LANES))
    gathered = lax.all_to_all(copies, "seq", 0, 0, tiled=True).reshape(seq_count * 8, LANES)
    mine = lax.all_gather(history, "x", axis=0)
    half = mine.shape[0] // 2
    theirs = [
        lax.ppermute(part, "core", [(0, 1), (1, 0)]) for part in (mine[:half], mine[half:])
    ]
    rows = mine.shape[0] * mine.shape[2]

    def project(side, *history):
        return pl.pallas_call(
            functools.partial(project_kernel, side),
            out_shape=(
                jax.ShapeDtypeStruct((users, rows, width), jnp.bfloat16),
                jax.ShapeDtypeStruct((users, width + ONES, rows), jnp.bfloat16),
            ),
            in_specs=[smem] + [vmem] * (len(history) + 2),
            out_specs=(vmem, vmem),
            compiler_params=pltpu.CompilerParams(vmem_limit_bytes=24 * 1024 * 1024),
            name="project",
        )(lengths, *history, w_key, w_value)

    keys0, values0 = project(0, mine)
    keys1, values1 = project(1, *theirs)
    partial = pl.pallas_call(
        attend_kernel,
        out_shape=jax.ShapeDtypeStruct((seq_count * SLOT, LANES), jnp.bfloat16),
        in_specs=[vmem] * 6,
        out_specs=vmem,
        scratch_shapes=[
            pltpu.VMEM((seq_count * 8, LANES), jnp.float32),
            pltpu.VMEM((seq_count * SLOT, LANES), jnp.float32),
        ],
        compiler_params=pltpu.CompilerParams(vmem_limit_bytes=32 * 1024 * 1024),
        name="attend",
    )(gathered, keys0, values0, keys1, values1, w_query)
    partial = partial.reshape(seq_count, SLOT // 2, 2, LANES)
    partial = lax.all_to_all(partial, "seq", 0, 0, tiled=True)
    return pl.pallas_call(
        join_kernel,
        out_shape=jax.ShapeDtypeStruct((users, own, width), jnp.bfloat16),
        in_specs=[vmem] * 3,
        out_specs=vmem,
        scratch_shapes=[pltpu.VMEM((seq_count * SLOT, LANES), jnp.float32)],
        compiler_params=pltpu.CompilerParams(vmem_limit_bytes=16 * 1024 * 1024),
        name="join",
    )(partial.reshape(seq_count * SLOT, LANES), norm_gain.reshape(1, width), w_out)


def solution(mesh):
    split = P(None, ("seq", "x", "core"), None)
    seq, cand = mesh.shape["seq"], mesh.shape["cand"]
    finer = Mesh(mesh.devices.reshape(seq, cand // 2, 2), ("seq", "x", "core"))
    return jax.shard_map(
        functools.partial(shards, seq),
        mesh=finer,
        in_specs=(split, split) + (P(),) * 6,
        out_specs=split,
        check_vma=False,
    )
```

```python
import functools
import math

import jax
import jax.numpy as jnp
from jax import lax
from jax.experimental import pallas as pl
from jax.experimental.pallas import tpu as pltpu
from jax.sharding import Mesh, PartitionSpec as P

HEAD_DIM = 32
LANES = 128
SLOT = 10
DEPTH = 16
FIRSTS = ((1, 12), (1, 4))
STATS = 64
EXPONENT = math.log2(math.e) / math.sqrt(HEAD_DIM)
NT = (((1,), (1,)), ((), ()))
ONES = 16


def parts_of(array, count):
    pieces = []
    for _ in range(count):
        piece = array.astype(jnp.bfloat16).astype(jnp.float32)
        pieces.append(piece)
        array = array - piece
    return pieces


def project_kernel(side, length_ref, *refs):
    history_refs, (wk_ref, wv_ref, gain_ref, keys_ref, values_ref, gain_out) = refs[:-6], refs[-6:]
    gain_out[...] = gain_ref[...]
    chips, users, block, width = history_refs[0].shape
    rows = len(history_refs) * chips * block
    first_row = lax.axis_index("seq") * 2 * rows
    core = (lax.axis_index("core") + side) % 2

    def position(shape, dimension):
        index = lax.broadcasted_iota(jnp.int32, shape, dimension)
        return (index // block) * (2 * block) + core * block + index % block

    row_index = position((rows, width), 0)
    lane_index = position((width + ONES, rows), 1)
    for user in range(users):
        valid = length_ref[user] - first_row
        history = jnp.concatenate(
            [ref[:, user].reshape(chips * block, width) for ref in history_refs], axis=0
        )
        keys = jnp.dot(history, wk_ref[...], preferred_element_type=jnp.float32)
        keys_ref[user] = jnp.where(row_index < valid, keys, keys[0:1]).astype(jnp.bfloat16)
        values = lax.dot_general(
            wv_ref[...], history, (((0,), (1,)), ((), ())), preferred_element_type=jnp.float32
        )
        values = jnp.concatenate([values, jnp.ones((ONES, rows), jnp.float32)], axis=0)
        values_ref[user] = jnp.where(lane_index < valid, values, 0.0).astype(jnp.bfloat16)


def attend_kernel(runs, cand_ref, keys0, values0, keys1, values1, wq_ref, out_ref, cand_wide, out_wide):
    users, _, width = keys0.shape
    devices = cand_ref.shape[0] // 8
    own = 2
    heads = width // HEAD_DIM
    cands = devices * own
    cand_wide[...] = cand_ref[...].astype(jnp.float32)
    head_of_lane = lax.broadcasted_iota(jnp.int32, (cands, width), 1) // HEAD_DIM
    for user in range(users):
        halves = [(keys0, values0), (keys1, values1)]
        any_valid = [values[user, width : width + 1, 0:1] > 0.0 for _, values in halves]
        keys = [
            jnp.where(any_valid[k], halves[k][0][user], halves[1 - k][0][user, 0:1])
            for k in range(2)
        ]
        candidates = [
            jnp.concatenate(
                [
                    jnp.concatenate(
                        [
                            cand_wide[pl.ds(8 * start + (user * own + i) * 2 + half, size, stride=8)]
                            for start, size in runs
                        ],
                        axis=0,
                    )
                    for half in range(2)
                ],
                axis=1,
            )
            for i in range(own)
        ]
        candidates = jnp.concatenate(candidates, axis=0).astype(jnp.bfloat16)
        queries = jnp.dot(candidates, wq_ref[...], preferred_element_type=jnp.float32)
        queries = queries.astype(jnp.bfloat16).astype(jnp.float32)
        numerators, peaks, totals = [], [], []
        for pair in range(heads // 2):
            both = jnp.concatenate(
                [
                    jnp.where(head_of_lane == 2 * pair + k, queries, 0.0).astype(jnp.bfloat16)
                    for k in range(2)
                ],
                axis=0,
            )
            scores = [
                lax.dot_general(part, both, NT, preferred_element_type=jnp.float32)
                for part in keys
            ]
            peak = jnp.max(jnp.maximum(scores[0], scores[1]), axis=0, keepdims=True)
            sums = 0.0
            for part, (_, values) in zip(scores, halves):
                exps = jnp.exp2((part - peak) * EXPONENT).astype(jnp.bfloat16)
                pair_values = jnp.concatenate(
                    [
                        values[user, 2 * pair * HEAD_DIM : 2 * (pair + 1) * HEAD_DIM],
                        values[user, width:],
                    ],
                    axis=0,
                )
                sums += jnp.dot(pair_values, exps, preferred_element_type=jnp.float32)
            for k in range(2):
                lanes = slice(k * cands, (k + 1) * cands)
                numerators.append(sums[k * HEAD_DIM : (k + 1) * HEAD_DIM, lanes])
                peaks.append(peak[:, lanes])
                totals.append(sums[2 * HEAD_DIM : 2 * HEAD_DIM + 1, lanes])
        total = jnp.concatenate(totals, axis=0)
        peak = jnp.where(total > 0.0, jnp.concatenate(peaks, axis=0), -1e30)
        pieces = parts_of(peak, 3) + parts_of(total, 2)
        filler = jnp.zeros((STATS - len(pieces) * heads, cands), jnp.float32)
        block = jnp.concatenate(numerators, axis=0)
        for half in range(2):
            turned = block[half * LANES : (half + 1) * LANES].T
            for i in range(own):
                row = (user * own + i) * 2 + half
                out_wide[pl.ds(row, devices, stride=SLOT), :] = turned[
                    i * devices : (i + 1) * devices
                ]
        stats = jnp.concatenate(pieces + [filler], axis=0)
        stats = jnp.concatenate(
            [stats[:, i * devices : (i + 1) * devices] for i in range(own)], axis=0
        )
        out_wide[pl.ds(2 * users * own + user, devices, stride=SLOT), :] = stats.T
    out_ref[...] = out_wide[...].astype(jnp.bfloat16)


def join_kernel(part_ref, gain_ref, wout_ref, out_ref, wide):
    width = wout_ref.shape[0]
    heads = width // HEAD_DIM
    devices = part_ref.shape[0] // SLOT
    users, own = out_ref.shape[:2]
    own_count = users * own
    wide[...] = part_ref[...].astype(jnp.float32)

    def rows(index):
        return wide[pl.ds(index, devices, stride=SLOT), :]

    lane = lax.broadcasted_iota(jnp.int32, (LANES, 2 * own * width), 0)
    column = lax.broadcasted_iota(jnp.int32, (LANES, 2 * own * width), 1)
    piece = lane % STATS // heads
    is_total = column // width % 2
    same = (
        (lane // STATS == column // (2 * width))
        & (lane % heads == column % width // HEAD_DIM)
        & (piece >= 3 * is_total)
        & (piece < 3 + 2 * is_total)
    )
    spread = jnp.where(same, 1.0, 0.0).astype(jnp.bfloat16)
    stats = jnp.concatenate([rows(2 * own_count + user) for user in range(users)], axis=0)
    stats = jnp.dot(stats.astype(jnp.bfloat16), spread, preferred_element_type=jnp.float32)
    attended = []
    for user in range(users):
        for i in range(own):
            both = stats[user * devices : (user + 1) * devices]
            peak = both[:, 2 * i * width : (2 * i + 1) * width]
            total = both[:, (2 * i + 1) * width : (2 * i + 2) * width]
            joint = jnp.max(peak, axis=0, keepdims=True)
            factor = jnp.exp2((peak - joint) * EXPONENT)
            index = 2 * (user * own + i)
            numerator = jnp.concatenate([rows(index), rows(index + 1)], axis=1)
            numerator = jnp.sum(numerator * factor, axis=0, keepdims=True)
            attended.append(numerator / jnp.sum(total * factor, axis=0, keepdims=True))
    attended = jnp.concatenate(attended, axis=0)
    normed = (
        attended
        * lax.rsqrt(jnp.mean(attended * attended, axis=-1, keepdims=True) + 1e-06)
        * gain_ref[...]
    )
    result = jnp.dot(
        normed.astype(jnp.bfloat16), wout_ref[...], preferred_element_type=jnp.float32
    )
    for user in range(users):
        out_ref[user] = result[user * own : (user + 1) * own].astype(jnp.bfloat16)


def seq_order(count, first):
    depth = math.gcd(count, DEPTH)
    breadth = count // depth
    return [
        [
            (y + first[0]) % breadth * depth + (z + first[1]) % depth
            for y in range(breadth)
            for z in range(depth)
        ]
    ]


def runs_of(given, wanted):
    runs = []
    for device in wanted:
        index = given.index(device)
        if runs and sum(runs[-1]) == index:
            runs[-1] = (runs[-1][0], runs[-1][1] + 1)
        else:
            runs.append((index, 1))
    return tuple(runs)


def shards(seq_count, candidates, history, lengths, w_query, w_key, w_value, norm_gain, w_out):
    users, own, width = candidates.shape
    there, back = (seq_order(seq_count, first) for first in FIRSTS)
    vmem = pl.BlockSpec(memory_space=pltpu.VMEM)
    smem = pl.BlockSpec(memory_space=pltpu.SMEM)
    copies = jnp.broadcast_to(candidates.reshape(1, 8, LANES), (seq_count, 8, LANES))
    gathered = lax.all_to_all(copies, "seq", 0, 0, axis_index_groups=there, tiled=True).reshape(seq_count * 8, LANES)
    mine = lax.all_gather(history, "x", axis=0)
    half = mine.shape[0] // 2
    theirs = [
        lax.ppermute(part, "core", [(0, 1), (1, 0)]) for part in (mine[:half], mine[half:])
    ]
    rows = mine.shape[0] * mine.shape[2]

    def project(side, gain, *history):
        return pl.pallas_call(
            functools.partial(project_kernel, side),
            out_shape=(
                jax.ShapeDtypeStruct((users, rows, width), jnp.bfloat16),
                jax.ShapeDtypeStruct((users, width + ONES, rows), jnp.bfloat16),
                jax.ShapeDtypeStruct((1, width), jnp.float32),
            ),
            in_specs=[smem] + [vmem] * (len(history) + 3),
            out_specs=(vmem, vmem, vmem),
            compiler_params=pltpu.CompilerParams(vmem_limit_bytes=24 * 1024 * 1024),
            name="project",
        )(lengths, *history, w_key, w_value, gain)

    keys0, values0, gain = project(0, norm_gain.reshape(1, width), mine)
    keys1, values1, gain = project(1, gain, *theirs)
    partial = pl.pallas_call(
        functools.partial(attend_kernel, runs_of(there[0], back[0])),
        out_shape=jax.ShapeDtypeStruct((seq_count * SLOT, LANES), jnp.bfloat16),
        in_specs=[vmem] * 6,
        out_specs=vmem,
        scratch_shapes=[
            pltpu.VMEM((seq_count * 8, LANES), jnp.float32),
            pltpu.VMEM((seq_count * SLOT, LANES), jnp.float32),
        ],
        compiler_params=pltpu.CompilerParams(vmem_limit_bytes=32 * 1024 * 1024),
        name="attend",
    )(gathered, keys0, values0, keys1, values1, w_query)
    partial = partial.reshape(seq_count, SLOT // 2, 2, LANES)
    partial = lax.all_to_all(partial, "seq", 0, 0, axis_index_groups=back, tiled=True)
    return pl.pallas_call(
        join_kernel,
        out_shape=jax.ShapeDtypeStruct((users, own, width), jnp.bfloat16),
        in_specs=[vmem] * 3,
        out_specs=vmem,
        scratch_shapes=[pltpu.VMEM((seq_count * SLOT, LANES), jnp.float32)],
        compiler_params=pltpu.CompilerParams(vmem_limit_bytes=16 * 1024 * 1024),
        name="join",
    )(partial.reshape(seq_count * SLOT, LANES), gain, w_out)


def solution(mesh):
    split = P(None, ("seq", "x", "core"), None)
    seq, cand = mesh.shape["seq"], mesh.shape["cand"]
    finer = Mesh(mesh.devices.reshape(seq, cand // 2, 2), ("seq", "x", "core"))
    return jax.shard_map(
        functools.partial(shards, seq),
        mesh=finer,
        in_specs=(split, split) + (P(),) * 6,
        out_specs=split,
        check_vma=False,
    )
```

```python
import functools
import math

import jax
import jax.numpy as jnp
from jax import lax
from jax.experimental import pallas as pl
from jax.experimental.pallas import tpu as pltpu
from jax.sharding import Mesh, PartitionSpec as P

HEAD_DIM = 32
LANES = 128
SLOT = 10
DEPTH = 16
FIRSTS = ((2, 12), (1, 4))
STATS = 64
EXPONENT = math.log2(math.e) / math.sqrt(HEAD_DIM)
NT = (((1,), (1,)), ((), ()))
ONES = 16


def parts_of(array, count):
    pieces = []
    for _ in range(count):
        piece = array.astype(jnp.bfloat16).astype(jnp.float32)
        pieces.append(piece)
        array = array - piece
    return pieces


def project_kernel(side, length_ref, *refs):
    if side:
        *refs, gain_ref, keys_ref, values_ref, gain_out = refs
        gain_out[...] = gain_ref[...]
    else:
        *refs, keys_ref, values_ref = refs
    *history_refs, wk_ref, wv_ref = refs
    chips, users, block, width = history_refs[0].shape
    rows = len(history_refs) * chips * block
    first_row = lax.axis_index("seq") * 2 * rows
    core = (lax.axis_index("core") + side) % 2

    def position(shape, dimension):
        index = lax.broadcasted_iota(jnp.int32, shape, dimension)
        return (index // block) * (2 * block) + core * block + index % block

    row_index = position((rows, width), 0)
    lane_index = position((width + ONES, rows), 1)
    for user in range(users):
        valid = length_ref[user] - first_row
        history = jnp.concatenate(
            [ref[:, user].reshape(chips * block, width) for ref in history_refs], axis=0
        )
        keys = jnp.dot(history, wk_ref[...], preferred_element_type=jnp.float32)
        keys_ref[user] = jnp.where(row_index < valid, keys, keys[0:1]).astype(jnp.bfloat16)
        values = lax.dot_general(
            wv_ref[...], history, (((0,), (1,)), ((), ())), preferred_element_type=jnp.float32
        )
        values = jnp.concatenate([values, jnp.ones((ONES, rows), jnp.float32)], axis=0)
        values_ref[user] = jnp.where(lane_index < valid, values, 0.0).astype(jnp.bfloat16)


def attend_kernel(runs, cand_ref, keys0, values0, keys1, values1, wq_ref, out_ref, cand_wide, out_wide):
    users, _, width = keys0.shape
    devices = cand_ref.shape[0] // 8
    own = 2
    heads = width // HEAD_DIM
    cands = devices * own
    cand_wide[...] = cand_ref[...].astype(jnp.float32)
    head_of_lane = lax.broadcasted_iota(jnp.int32, (cands, width), 1) // HEAD_DIM
    all_keys, all_queries = [], []
    for user in range(users):
        halves = [(keys0, values0), (keys1, values1)]
        any_valid = [values[user, width : width + 1, 0:1] > 0.0 for _, values in halves]
        keys = [
            jnp.where(any_valid[k], halves[k][0][user], halves[1 - k][0][user, 0:1])
            for k in range(2)
        ]
        candidates = [
            jnp.concatenate(
                [
                    jnp.concatenate(
                        [
                            cand_wide[pl.ds(8 * start + (user * own + i) * 2 + half, size, stride=8)]
                            for start, size in runs
                        ],
                        axis=0,
                    )
                    for half in range(2)
                ],
                axis=1,
            )
            for i in range(own)
        ]
        candidates = jnp.concatenate(candidates, axis=0).astype(jnp.bfloat16)
        queries = jnp.dot(candidates, wq_ref[...], preferred_element_type=jnp.float32)
        queries = queries.astype(jnp.bfloat16).astype(jnp.float32)
        all_keys.append(keys)
        all_queries.append(queries)

    def scores_of(user, pair):
        both = jnp.concatenate(
            [
                jnp.where(head_of_lane == 2 * pair + k, all_queries[user], 0.0).astype(jnp.bfloat16)
                for k in range(2)
            ],
            axis=0,
        )
        return [
            lax.dot_general(part, both, NT, preferred_element_type=jnp.float32)
            for part in all_keys[user]
        ]

    steps = [(user, pair) for user in range(users) for pair in range(heads // 2)]
    ahead = [scores_of(*step) for step in steps[:2]]
    for step, (user, pair) in enumerate(steps):
        if step + 2 < len(steps):
            ahead.append(scores_of(*steps[step + 2]))
        scores = ahead.pop(0)
        halves = [(keys0, values0), (keys1, values1)]
        if pair == 0:
            numerators, peaks, totals = [], [], []
        peak = jnp.max(jnp.maximum(scores[0], scores[1]), axis=0, keepdims=True)
        sums = 0.0
        for part, (_, values) in zip(scores, halves):
            exps = jnp.exp2((part - peak) * EXPONENT).astype(jnp.bfloat16)
            pair_values = jnp.concatenate(
                [
                    values[user, 2 * pair * HEAD_DIM : 2 * (pair + 1) * HEAD_DIM],
                    values[user, width:],
                ],
                axis=0,
            )
            sums += jnp.dot(pair_values, exps, preferred_element_type=jnp.float32)
        for k in range(2):
            lanes = slice(k * cands, (k + 1) * cands)
            numerators.append(sums[k * HEAD_DIM : (k + 1) * HEAD_DIM, lanes])
            peaks.append(peak[:, lanes])
            totals.append(sums[2 * HEAD_DIM : 2 * HEAD_DIM + 1, lanes])
        if pair < heads // 2 - 1:
            continue
        total = jnp.concatenate(totals, axis=0)
        peak = jnp.where(total > 0.0, jnp.concatenate(peaks, axis=0), -1e30)
        pieces = parts_of(peak, 3) + parts_of(total, 2)
        filler = jnp.zeros((STATS - len(pieces) * heads, cands), jnp.float32)
        block = jnp.concatenate(numerators, axis=0)
        for half in range(2):
            turned = block[half * LANES : (half + 1) * LANES].T
            for i in range(own):
                row = (user * own + i) * 2 + half
                out_wide[pl.ds(row, devices, stride=SLOT), :] = turned[
                    i * devices : (i + 1) * devices
                ]
        stats = jnp.concatenate(pieces + [filler], axis=0)
        stats = jnp.concatenate(
            [stats[:, i * devices : (i + 1) * devices] for i in range(own)], axis=0
        )
        out_wide[pl.ds(2 * users * own + user, devices, stride=SLOT), :] = stats.T
    out_ref[...] = out_wide[...].astype(jnp.bfloat16)


def join_kernel(part_ref, gain_ref, wout_ref, out_ref, wide):
    width = wout_ref.shape[0]
    heads = width // HEAD_DIM
    devices = part_ref.shape[0] // SLOT
    users, own = out_ref.shape[:2]
    own_count = users * own
    wide[...] = part_ref[...].astype(jnp.float32)

    def rows(index):
        return wide[pl.ds(index, devices, stride=SLOT), :]

    lane = lax.broadcasted_iota(jnp.int32, (LANES, 2 * own * width), 0)
    column = lax.broadcasted_iota(jnp.int32, (LANES, 2 * own * width), 1)
    piece = lane % STATS // heads
    is_total = column // width % 2
    same = (
        (lane // STATS == column // (2 * width))
        & (lane % heads == column % width // HEAD_DIM)
        & (piece >= 3 * is_total)
        & (piece < 3 + 2 * is_total)
    )
    spread = jnp.where(same, 1.0, 0.0).astype(jnp.bfloat16)
    stats = jnp.concatenate([rows(2 * own_count + user) for user in range(users)], axis=0)
    stats = jnp.dot(stats.astype(jnp.bfloat16), spread, preferred_element_type=jnp.float32)
    attended = []
    for user in range(users):
        for i in range(own):
            both = stats[user * devices : (user + 1) * devices]
            peak = both[:, 2 * i * width : (2 * i + 1) * width]
            total = both[:, (2 * i + 1) * width : (2 * i + 2) * width]
            joint = jnp.max(peak, axis=0, keepdims=True)
            factor = jnp.exp2((peak - joint) * EXPONENT)
            index = 2 * (user * own + i)
            numerator = jnp.concatenate([rows(index), rows(index + 1)], axis=1)
            numerator = jnp.sum(numerator * factor, axis=0, keepdims=True)
            attended.append(numerator / jnp.sum(total * factor, axis=0, keepdims=True))
    attended = jnp.concatenate(attended, axis=0)
    normed = (
        attended
        * lax.rsqrt(jnp.mean(attended * attended, axis=-1, keepdims=True) + 1e-06)
        * gain_ref[...]
    )
    result = jnp.dot(
        normed.astype(jnp.bfloat16), wout_ref[...], preferred_element_type=jnp.float32
    )
    for user in range(users):
        out_ref[user] = result[user * own : (user + 1) * own].astype(jnp.bfloat16)


def seq_order(count, first):
    depth = math.gcd(count, DEPTH)
    breadth = count // depth
    return [
        [
            (y + first[0]) % breadth * depth + (z + first[1]) % depth
            for y in range(breadth)
            for z in range(depth)
        ]
    ]


def runs_of(given, wanted):
    runs = []
    for device in wanted:
        index = given.index(device)
        if runs and sum(runs[-1]) == index:
            runs[-1] = (runs[-1][0], runs[-1][1] + 1)
        else:
            runs.append((index, 1))
    return tuple(runs)


def shards(seq_count, candidates, history, lengths, w_query, w_key, w_value, norm_gain, w_out):
    users, own, width = candidates.shape
    there, back = (seq_order(seq_count, first) for first in FIRSTS)
    vmem = pl.BlockSpec(memory_space=pltpu.VMEM)
    smem = pl.BlockSpec(memory_space=pltpu.SMEM)
    copies = jnp.broadcast_to(candidates.reshape(1, 8, LANES), (seq_count, 8, LANES))
    gathered = lax.all_to_all(copies, "seq", 0, 0, axis_index_groups=there, tiled=True).reshape(seq_count * 8, LANES)
    mine = lax.all_gather(history, "x", axis=0)
    half = mine.shape[0] // 2
    theirs = [
        lax.ppermute(part, "core", [(0, 1), (1, 0)]) for part in (mine[:half], mine[half:])
    ]
    rows = mine.shape[0] * mine.shape[2]

    def project(side, *operands):
        shapes = [
            jax.ShapeDtypeStruct((users, rows, width), jnp.bfloat16),
            jax.ShapeDtypeStruct((users, width + ONES, rows), jnp.bfloat16),
        ]
        if side:
            shapes.append(jax.ShapeDtypeStruct((1, width), jnp.float32))
        return pl.pallas_call(
            functools.partial(project_kernel, side),
            out_shape=shapes,
            in_specs=[smem] + [vmem] * len(operands),
            out_specs=[vmem] * len(shapes),
            compiler_params=pltpu.CompilerParams(vmem_limit_bytes=24 * 1024 * 1024),
            name="project",
        )(lengths, *operands)

    keys0, values0 = project(0, mine, w_key, w_value)
    keys1, values1, gain = project(1, *theirs, w_key, w_value, norm_gain.reshape(1, width))
    partial = pl.pallas_call(
        functools.partial(attend_kernel, runs_of(there[0], back[0])),
        out_shape=jax.ShapeDtypeStruct((seq_count * SLOT, LANES), jnp.bfloat16),
        in_specs=[vmem] * 6,
        out_specs=vmem,
        scratch_shapes=[
            pltpu.VMEM((seq_count * 8, LANES), jnp.float32),
            pltpu.VMEM((seq_count * SLOT, LANES), jnp.float32),
        ],
        compiler_params=pltpu.CompilerParams(vmem_limit_bytes=32 * 1024 * 1024),
        name="attend",
    )(gathered, keys0, values0, keys1, values1, w_query)
    partial = partial.reshape(seq_count, SLOT // 2, 2, LANES)
    partial = lax.all_to_all(partial, "seq", 0, 0, axis_index_groups=back, tiled=True)
    return pl.pallas_call(
        join_kernel,
        out_shape=jax.ShapeDtypeStruct((users, own, width), jnp.bfloat16),
        in_specs=[vmem] * 3,
        out_specs=vmem,
        scratch_shapes=[pltpu.VMEM((seq_count * SLOT, LANES), jnp.float32)],
        compiler_params=pltpu.CompilerParams(vmem_limit_bytes=16 * 1024 * 1024),
        name="join",
    )(partial.reshape(seq_count * SLOT, LANES), gain, w_out)


def solution(mesh):
    split = P(None, ("seq", "x", "core"), None)
    seq, cand = mesh.shape["seq"], mesh.shape["cand"]
    finer = Mesh(mesh.devices.reshape(seq, cand // 2, 2), ("seq", "x", "core"))
    return jax.shard_map(
        functools.partial(shards, seq),
        mesh=finer,
        in_specs=(split, split) + (P(),) * 6,
        out_specs=split,
        check_vma=False,
    )
```
